256 devices in a mesh: dimer: 8 (over y_hi, x), grid: 32 (over z, y_lo, core).
Axes of the slice: x: 4, y: 4 (y_hi: 2, y_lo: 2; y = y_hi * 2 + y_lo), z: 8, core: 2. Of those that a mesh axis runs over, the one named last changes fastest.
Arguments:
- basis_values: bfloat16 [8, 40960, 1024], P('dimer', 'grid'), may hold values from -15 to 15
- aux_values: bfloat16 [8, 40960, 2048], P('dimer', 'grid'), may hold values from -6 to 6
- factors: bfloat16 [8, 512, 128], P('dimer', 'grid'), may hold values from -0.25 to 0.25
- frag_slot: int32 [8], replicated, may hold values from 0 to 7, each once
- dimer_pairs: int32 [8, 2], P('dimer'), may hold values from 0 to 7, as said below
- counts: int32 [8, 32], P('dimer', 'grid'), may hold values from 1 to 1280, 16384 in all within a row
- weights: float32 [8, 40960], P('dimer', 'grid'), may hold values from 0.000390625 to 0.0015625
- metric_inv: float32 [8, 2048, 2048], P('dimer', 'grid'), may hold values from -1 to 1, as said below
Outputs:
- frag_fock: float32 [8, 512, 512], P('dimer', 'grid')
- coupling: float32 [8, 512, 512], P('dimer', 'grid')
The draws below stay inside these ranges and needn't reach their ends.
Inputs may be any that keep to these rules, and one draw needn't show every extreme that they name: `dimer_pairs`: each fragment is named by exactly two dimers, and the two fragments of a dimer differ. For each dimer the 32 counts sum to 16384 and the largest equals 1280. `metric_inv`: each matrix is symmetric.
All inputs are finite; a program needn't handle non-finite values. No bound on the sum of `counts` on one device may be relied on, other than what follows from the above.
Results may differ from the reference program's by a relative error of at most 0.0029.
Values may be sent and summed in bfloat16 or wider, within the bound.
A program may use at most 64 MiB of HBM per device.

```python
import math
import jax
import jax.numpy as jnp
import numpy as np
from jax import lax

NB_F = 512
NOCC = 128
NAUX = 2048
PTS_DEV = 1280
NB = 1024
NDIMER = 8
NFRAG = 8
NPTS = 40960
LIVE = 16384
N_GRID = 32


def draw_dimer_pairs(key, part):
    order = jax.random.permutation(key, NFRAG).astype(jnp.int32)
    return jnp.stack([order, jnp.roll(order, -1)], axis=1)


def draw_basis_values(key, part):
    key_values, key_scale = jax.random.split(key)
    values = jax.random.truncated_normal(key_values, -5.0, 5.0, (NDIMER, NPTS, NB), jnp.float32)
    row_scale = jnp.exp(jax.random.uniform(key_scale, (NDIMER, NPTS, 1), jnp.float32, math.log(0.3), math.log(3.0)))
    return (values * row_scale).astype(jnp.bfloat16)


def draw_metric_inv(key, part):
    key_off, key_diag = jax.random.split(key)
    raw = jax.random.truncated_normal(key_off, -4.0, 4.0, (NDIMER, NAUX, NAUX), jnp.float32)
    symmetric = (raw + jnp.swapaxes(raw, 1, 2)) * (0.7 / NAUX)
    diagonal = jax.random.uniform(key_diag, (NDIMER, NAUX), jnp.float32, 2.0, 4.0)
    identity = jnp.eye(NAUX, dtype=jnp.float32)
    return symmetric + diagonal[:, :, None] * identity[None, :, :] * NAUX ** (-0.5)


def levels(stream_key, extent, cuts, least, high):
    level = 1.0
    for axis_at, blocks in cuts:
        heights = jax.random.uniform(jax.random.fold_in(jax.random.fold_in(stream_key, 6), axis_at), (blocks,), jnp.float32, least / len(cuts), high / len(cuts))
        level = level * jnp.repeat(jnp.exp(heights), extent[axis_at] // blocks).reshape((-1,) + (1,) * (len(extent) - 1 - axis_at))
    return level


def length_profile(amount, total, most, lean):
    loads = [(1 << 20) // math.isqrt(rank ** lean) + 1 for rank in range(2, amount + 1)]
    surplus, given = total - most - (amount - 1), [1] * (amount - 1)
    while surplus > 0:
        candidates = [i for i in range(amount - 1) if given[i] < most]
        mass, left = sum([loads[i] for i in candidates]), surplus
        for i in candidates:
            addition = min(most - given[i], max(1, left * loads[i] // mass), surplus)
            given[i] = given[i] + addition
            surplus = surplus - addition
    return np.array([most] + given)


def uneven_parts(stream_key, count, total, bound, slope):
    if count == 2:
        one = jax.random.randint(stream_key, (), max(1, total - bound), min(bound, total - 1) + 1)
        return jnp.stack([one, total - one])
    lengths = jnp.asarray(length_profile(count, total, bound, slope), jnp.int32)
    couples = (count - 1) // 2
    source_of, receiver = lengths[1:1 + 2 * couples:2], lengths[2:2 + 2 * couples:2]
    room = jnp.minimum(source_of - 1, bound - receiver)
    shifted = jax.random.randint(jax.random.fold_in(stream_key, 1), (couples,), 0, 1 << 20) % (room + 1)
    lengths = lengths.at[1:1 + 2 * couples:2].set(source_of - shifted).at[2:2 + 2 * couples:2].set(receiver + shifted)
    return lengths[jax.random.permutation(jax.random.fold_in(stream_key, 2), count)]


def bell_draw(rng, shape, scale, bound, shards=(), kind=jnp.bfloat16):
    factor_of = levels(rng, shape, shards, -0.22, 0.18) if shards else 1.0
    entries = jax.random.normal(rng, shape, jnp.float32) * scale * factor_of
    return jnp.minimum(jnp.maximum(entries, -bound), bound).astype(kind)


def setup_inputs(seed: int = 0) -> dict:
    splits = jax.random.split(jax.random.key(seed), 9)
    return {
        "basis_values": draw_basis_values(jax.random.fold_in(splits[8], 71), 0),
        "aux_values": bell_draw(splits[1], (NDIMER, NPTS, NAUX), 1.0, 6.0, ((0, 8), (1, 32))),
        "factors": bell_draw(splits[2], (NFRAG, NB_F, NOCC), NB_F ** -0.5, 0.25, ((0, 8), (1, 32))),
        "frag_slot": jax.random.permutation(splits[3], NFRAG).astype(jnp.int32),
        "dimer_pairs": draw_dimer_pairs(jax.random.fold_in(splits[8], 71), 0),
        "counts": jax.vmap(lambda own: uneven_parts(own, N_GRID, LIVE, PTS_DEV, 2))(jax.random.split(splits[5], NDIMER)).reshape((NDIMER, N_GRID)).astype(jnp.int32),
        "weights": jnp.clip(jnp.exp(math.log(0.0015625) - 1.3862944 * jax.random.uniform(splits[6], (NDIMER, NPTS), jnp.float32) ** levels(splits[6], (NDIMER, NPTS), ((0, 8), (1, 32)), -0.2, 0.2)), 0.000390625, 0.0015625),
        "metric_inv": draw_metric_inv(jax.random.fold_in(splits[8], 71), 0),
    }


exchange_coeff = 0.9847450218426964


def reference(basis_values, aux_values, factors, frag_slot, dimer_pairs, counts, weights, metric_inv):
    highest = lax.Precision.HIGHEST
    frag_fock = jnp.zeros((NFRAG, NB_F, NB_F), jnp.float32)
    couplings = []
    position = jnp.arange(NPTS, dtype=jnp.int32)
    owner_device = position // PTS_DEV
    offset = position % PTS_DEV
    for dimer_index in range(NDIMER):
        basis_rows = basis_values[dimer_index]
        aux_float = aux_values[dimer_index].astype(jnp.float32)
        live_weight = jnp.where(offset < counts[dimer_index][owner_device], weights[dimer_index], jnp.zeros((), jnp.float32))
        first_factor = factors[frag_slot[dimer_pairs[dimer_index, 0]]]
        second_factor = factors[frag_slot[dimer_pairs[dimer_index, 1]]]
        orb_first = jnp.dot(basis_rows[:, :NB_F], first_factor, preferred_element_type=jnp.float32)
        orb_second = jnp.dot(basis_rows[:, NB_F:], second_factor, preferred_element_type=jnp.float32)
        density = (jnp.sum(orb_first * orb_first, axis=1) + jnp.sum(orb_second * orb_second, axis=1)) / (2.0 * NOCC)
        exchange = -exchange_coeff * jnp.cbrt(density)
        fitted = jnp.dot(live_weight * density, aux_float, precision=highest)
        coefficients = jnp.dot(metric_inv[dimer_index], fitted, precision=highest)
        coulomb = jnp.dot(aux_float, coefficients, precision=highest)
        average = jnp.sum(live_weight * (coulomb + exchange)) / jnp.sum(live_weight)
        potential = live_weight * (coulomb + exchange - average)
        weighted_basis = (basis_rows * potential[:, None]).astype(jnp.bfloat16)
        dimer_fock = lax.dot_general(weighted_basis, basis_rows, (((0,), (0,)), ((), ())), preferred_element_type=jnp.float32)
        frag_fock = frag_fock.at[dimer_pairs[dimer_index, 0]].add(dimer_fock[:NB_F, :NB_F])
        frag_fock = frag_fock.at[dimer_pairs[dimer_index, 1]].add(dimer_fock[NB_F:, NB_F:])
        couplings.append(dimer_fock[:NB_F, NB_F:])
    return frag_fock, jnp.stack(couplings)
```

```python
import functools

import jax
import jax.numpy as jnp
from jax import lax
from jax.experimental import pallas as pl
from jax.experimental.pallas import tpu as pltpu
from jax.sharding import PartitionSpec as P

EXCHANGE_COEFF = 0.9847450218426964
GRID = 32
DIMERS = 8
CHIPS = 16
PTS = 1280
FB = 512
OCC = 128
AUX = 2048
F32 = jnp.float32
BF16 = jnp.bfloat16
MESH = pl.DeviceIdType.MESH


def wait_bytes(ref, sem):
    pltpu.make_async_copy(ref, ref, sem).wait()


def remote(src, dst, send_sem, recv_sem, axis, index):
    copy = pltpu.make_async_remote_copy(
        src_ref=src,
        dst_ref=dst,
        send_sem=send_sem,
        recv_sem=recv_sem,
        device_id={axis: index},
        device_id_type=MESH,
    )
    copy.start()


def hi_lo_rows(row):
    high = row.astype(BF16)
    low = (row - high.astype(F32)).astype(BF16)
    which = lax.broadcasted_iota(jnp.int32, (16, row.shape[1]), 0)
    zero = jnp.zeros((16, row.shape[1]), F32)
    high, low = high.astype(F32), low.astype(F32)
    return jnp.where(which == 0, high, jnp.where(which == 1, low, zero)).astype(BF16)


def cube_root(x):
    safe = jnp.where(x > 0, x, 1.0)
    y = jnp.exp(jnp.log(safe) * (1.0 / 3.0))
    y = y - (y - safe / (y * y)) * (1.0 / 3.0)
    return jnp.where(x > 0, y, 0.0)


def dot(a, b):
    return jnp.dot(a, b, preferred_element_type=F32)


def kernel(
    basis_hbm, aux_hbm, fac_ref, slot_ref, pairs_ref, counts_ref, weights_ref, metric_hbm,
    frag_out, coup_out,
    b, aux, bt, wt, mbuf, facbuf, facsend, facall,
    ssend, srecv, fsend, frecv, csend, crecv,
    acc, core_send, core_recv, y_send, y_recv, z_send, z_recv, d_send, d_recv,
    local_sem, fa_sem, fb_sem, fc_sem, m_sem, s_sem, f_sem, c_sem,
    core_sem, y_sem, z_sem, d_sem,
):
    d = lax.axis_index("dimer")
    g = lax.axis_index("grid")
    core = lax.rem(g, 2)
    chip = g // 2
    y = lax.rem(chip, 2)
    z = chip // 2
    other_core = g + 1 - 2 * core
    other_y = g + 2 - 4 * y

    load_b = pltpu.make_async_copy(basis_hbm.at[0], b, local_sem.at[0])
    load_aux = pltpu.make_async_copy(aux_hbm.at[0], aux, local_sem.at[1])
    load_m = pltpu.make_async_copy(metric_hbm.at[0], mbuf.at[core], local_sem.at[2])
    load_b.start()
    load_aux.start()
    load_m.start()

    barrier = pltpu.get_barrier_semaphore()
    for k in range(1, GRID):
        pl.semaphore_signal(
            barrier, inc=1, device_id={"grid": lax.rem(g + k, GRID)}, device_id_type=MESH
        )
    for k in range(1, DIMERS):
        pl.semaphore_signal(
            barrier, inc=1, device_id={"dimer": lax.rem(d + k, DIMERS)}, device_id_type=MESH
        )
    pl.semaphore_wait(barrier, GRID - 1 + DIMERS - 1)

    for k in range(1, DIMERS):
        remote(
            fac_ref.at[0], facbuf.at[d], fa_sem.at[0], fa_sem.at[1],
            "dimer", lax.rem(d + k, DIMERS),
        )
    facbuf[d] = fac_ref[0]
    remote(metric_hbm.at[0], mbuf.at[core], m_sem.at[0], m_sem.at[1], "grid", other_core)

    load_b.wait()
    for block in range(8):
        turned = b[:, block * 128:(block + 1) * 128].T
        for part in range(8):
            group = block * 8 + part
            half, owner = group // 32, group % 32
            place = half * 32 + (owner % 2) * 16 + ((owner // 2) % 2) * 8 + owner // 4
            bt[place * 16:(place + 1) * 16, :] = turned[part * 16:(part + 1) * 16, :]

    first, second = pairs_ref[0, 0], pairs_ref[0, 1]
    place = core * 256 + y * 128 + z * 16
    rows = pl.ds(pl.multiple_of(place, 16), 16)
    wait_bytes(facbuf.at[pl.ds(0, DIMERS - 1)], fa_sem.at[1])
    facsend[0] = facbuf[slot_ref[first]]
    facsend[1] = facbuf[slot_ref[second]]
    facall[:, rows, :] = facsend[...]
    for k in range(1, CHIPS):
        remote(
            facsend, facall.at[:, rows, :], fb_sem.at[0], fb_sem.at[1],
            "grid", 2 * lax.rem(chip + k, CHIPS) + core,
        )

    position = lax.broadcasted_iota(jnp.int32, (1, PTS), 1)
    lw = jnp.where(position < counts_ref[0, 0], weights_ref[...], 0.0)
    load_aux.wait()
    sums = dot(hi_lo_rows(lw), aux[...])
    sums = sums[0:1, :] + sums[1:2, :]
    for k in range(CHIPS):
        ssend[k] = sums[:, k * 128:(k + 1) * 128]
    srecv[g] = ssend[chip]
    for k in range(1, GRID):
        to = lax.rem(g + k, GRID)
        remote(ssend.at[to // 2], srecv.at[g], s_sem.at[0], s_sem.at[1], "grid", to)

    wait_bytes(facall.at[:, pl.ds(0, 240), :], fb_sem.at[1])
    own_half = pl.ds(pl.multiple_of(core * 256, 256), 256)
    remote(
        facall.at[:, own_half, :], facall.at[:, own_half, :], fc_sem.at[0], fc_sem.at[1],
        "grid", other_core,
    )
    wait_bytes(facall.at[:, pl.ds(0, 256), :], fc_sem.at[1])

    turn = (((0,), (0,)), ((), ()))
    density = jnp.zeros((1, PTS), F32)
    for half in range(2):
        orbitals = lax.dot_general(
            facall[half], bt[half * FB:(half + 1) * FB, :], turn, preferred_element_type=F32
        )
        density += jnp.sum(orbitals * orbitals, axis=0, keepdims=True)
    density = density * (1.0 / (2.0 * OCC))
    exchange = -EXCHANGE_COEFF * cube_root(density)

    fitted = dot(hi_lo_rows(lw * density), aux[...])
    fsend[...] = fitted[0:1, :] + fitted[1:2, :]
    frecv[chip] = fsend[...]
    for k in range(1, CHIPS):
        remote(
            fsend, frecv.at[chip], f_sem.at[0], f_sem.at[1],
            "grid", 2 * lax.rem(chip + k, CHIPS) + core,
        )
    local_exchange = jnp.sum(lw * exchange, axis=1, keepdims=True)
    local_weight = jnp.sum(lw, axis=1, keepdims=True)
    wait_bytes(srecv.at[pl.ds(0, GRID - 1)], s_sem.at[1])
    s_total = jnp.sum(srecv[...], axis=0)
    load_m.wait()
    wait_bytes(mbuf.at[0], m_sem.at[1])
    wait_bytes(frecv.at[pl.ds(0, CHIPS - 1)], f_sem.at[1])
    own_fitted = jnp.sum(frecv[...], axis=0)

    rows_m = jnp.concatenate([mbuf[0], mbuf[1]], axis=0)
    terms = rows_m[:, 0:128] * own_fitted[:, 0:128]
    for k in range(1, CHIPS):
        cols = slice(k * 128, (k + 1) * 128)
        terms += rows_m[:, cols] * own_fitted[:, cols]
    coef_part = jnp.sum(terms.T, axis=0, keepdims=True)
    total_part = jnp.sum(coef_part * s_total, axis=1, keepdims=True) + local_exchange
    lane = lax.broadcasted_iota(jnp.int32, (1, 128), 1)
    csend[0:1, :] = coef_part
    csend[1:2, :] = jnp.where(lane == 0, total_part, jnp.where(lane == 1, local_weight, 0.0))
    crecv[g] = csend[...]
    for k in range(1, GRID):
        remote(
            csend, crecv.at[g], c_sem.at[0], c_sem.at[1], "grid", lax.rem(g + k, GRID)
        )
    wait_bytes(crecv.at[pl.ds(0, GRID - 1)], c_sem.at[1])

    totals = jnp.sum(crecv[...], axis=0)[1:2, :]
    average = totals[:, 0:1] / totals[:, 1:2]
    coefficients = jnp.concatenate(
        [crecv[2 * k, 0:1, :] + crecv[2 * k + 1, 0:1, :] for k in range(CHIPS)], axis=1
    )
    numbers = (((1,), (1,)), ((), ()))
    coulomb = lax.dot_general(
        hi_lo_rows(coefficients), aux[...], numbers, preferred_element_type=F32
    )
    coulomb = coulomb[0:1, :] + coulomb[1:2, :]
    potential = lw * (coulomb + exchange - average)
    wt[...] = (bt[...].astype(F32) * potential).astype(BF16)

    blocks = ((0, 0), (1, 1), (0, 1))

    def product(block, of_core):
        half, column = blocks[block]
        at = pl.ds(pl.multiple_of(half * FB + of_core * 256, 256), 256)
        return dot(wt[at, :], b[:, column * FB:(column + 1) * FB])

    def core_stage(block):
        core_send[block] = product(block, 1 - core)
        remote(
            core_send.at[block], core_recv.at[block],
            core_sem.at[0, block], core_sem.at[1, block], "grid", other_core,
        )
        acc[block] = product(block, core)

    def y_stage(block):
        wait_bytes(core_recv.at[block], core_sem.at[1, block])
        there = pl.ds(pl.multiple_of((1 - y) * 128, 128), 128)
        y_send[block] = (acc[block, there, :] + core_recv[block, there, :]).astype(BF16)
        remote(
            y_send.at[block], y_recv.at[block],
            y_sem.at[0, block], y_sem.at[1, block], "grid", other_y,
        )

    def z_stage(block):
        here = pl.ds(pl.multiple_of(y * 128, 128), 128)
        own = acc[block, here, :] + core_recv[block, here, :]
        wait_bytes(y_recv.at[block], y_sem.at[1, block])
        own = own + y_recv[block].astype(F32)
        acc[block, pl.ds(0, 128), :] = own
        z_send[block] = own.astype(BF16)
        for k in range(1, 8):
            to = lax.rem(z + k, 8)
            at = pl.ds(pl.multiple_of(to * 16, 16), 16)
            remote(
                z_send.at[block, at, :], z_recv.at[block, k - 1],
                z_sem.at[0, block], z_sem.at[1, block], "grid", to * 4 + y * 2 + core,
            )

    def shares(block):
        at = pl.ds(pl.multiple_of(z * 16, 16), 16)
        own = acc[block, at, :]
        wait_bytes(z_recv.at[block], z_sem.at[1, block])
        for k in range(7):
            own = own + z_recv[block, k].astype(F32)
        return own

    core_stage(0)
    core_stage(1)
    y_stage(0)
    core_stage(2)
    y_stage(1)
    y_stage(2)
    z_stage(0)
    z_stage(1)
    z_stage(2)
    own_first = shares(0)
    own_second = shares(1)

    def for_fragment(index):
        return jnp.where(first == index, own_first, 0.0) + jnp.where(
            second == index, own_second, 0.0
        )

    for k in range(1, DIMERS):
        to = lax.rem(d + k, DIMERS)
        d_send[k - 1] = for_fragment(to)
        remote(
            d_send.at[k - 1], d_recv.at[k - 1], d_sem.at[0], d_sem.at[1], "dimer", to
        )
    own = for_fragment(d)
    coup_out[0] = shares(2)
    wait_bytes(d_recv, d_sem.at[1])
    for k in range(DIMERS - 1):
        own = own + d_recv[k]
    frag_out[0] = own

    wait_bytes(facbuf.at[pl.ds(0, DIMERS - 1)], fa_sem.at[0])
    wait_bytes(mbuf.at[0], m_sem.at[0])
    wait_bytes(facall.at[:, pl.ds(0, 240), :], fb_sem.at[0])
    wait_bytes(facall.at[:, pl.ds(0, 256), :], fc_sem.at[0])
    wait_bytes(srecv.at[pl.ds(0, GRID - 1)], s_sem.at[0])
    wait_bytes(frecv.at[pl.ds(0, CHIPS - 1)], f_sem.at[0])
    wait_bytes(crecv.at[pl.ds(0, GRID - 1)], c_sem.at[0])
    for block in range(3):
        wait_bytes(core_recv.at[block], core_sem.at[0, block])
        wait_bytes(y_recv.at[block], y_sem.at[0, block])
        wait_bytes(z_recv.at[block], z_sem.at[0, block])
    wait_bytes(d_recv, d_sem.at[0])


def shards(basis_values, aux_values, factors, frag_slot, dimer_pairs, counts, weights, metric_inv):
    vmem = pl.BlockSpec(memory_space=pltpu.VMEM)
    smem = pl.BlockSpec(memory_space=pltpu.SMEM)
    hbm = pl.BlockSpec(memory_space=pl.ANY)
    dma = pltpu.SemaphoreType.DMA
    share = jax.ShapeDtypeStruct((1, FB // GRID, FB), F32)
    return pl.pallas_call(
        kernel,
        name="fock",
        out_shape=(share, share),
        in_specs=[hbm, hbm, vmem, smem, smem, smem, vmem, hbm],
        out_specs=(vmem, vmem),
        scratch_shapes=[
            pltpu.VMEM((PTS, 2 * FB), BF16),
            pltpu.VMEM((PTS, AUX), BF16),
            pltpu.VMEM((2 * FB, PTS), BF16),
            pltpu.VMEM((2 * FB, PTS), BF16),
            pltpu.VMEM((2, AUX // GRID, AUX), F32),
            pltpu.VMEM((DIMERS, FB // GRID, OCC), BF16),
            pltpu.VMEM((2, FB // GRID, OCC), BF16),
            pltpu.VMEM((2, FB, OCC), BF16),
            pltpu.VMEM((CHIPS, 1, 128), F32),
            pltpu.VMEM((GRID, 1, 128), F32),
            pltpu.VMEM((1, AUX), F32),
            pltpu.VMEM((CHIPS, 1, AUX), F32),
            pltpu.VMEM((2, 128), F32),
            pltpu.VMEM((GRID, 2, 128), F32),
            pltpu.VMEM((3, 256, FB), F32),
            pltpu.VMEM((3, 256, FB), F32),
            pltpu.VMEM((3, 256, FB), F32),
            pltpu.VMEM((3, 128, FB), BF16),
            pltpu.VMEM((3, 128, FB), BF16),
            pltpu.VMEM((3, 128, FB), BF16),
            pltpu.VMEM((3, 7, 16, FB), BF16),
            pltpu.VMEM((DIMERS - 1, 16, FB), F32),
            pltpu.VMEM((DIMERS - 1, 16, FB), F32),
            dma((3,)), dma((2,)), dma((2,)), dma((2,)), dma((2,)), dma((2,)), dma((2,)), dma((2,)),
            dma((2, 3)), dma((2, 3)), dma((2, 3)), dma((2,)),
        ],
        compiler_params=pltpu.CompilerParams(
            collective_id=0, has_side_effects=True, vmem_limit_bytes=60 * 1024 * 1024
        ),
        cost_estimate=pl.CostEstimate(
            flops=2 * PTS * (2 * FB * OCC + 3 * AUX + 3 * FB * FB),
            bytes_accessed=2 * PTS * (2 * FB + AUX) + 4 * AUX * AUX // GRID,
            transcendentals=2 * PTS,
        ),
    )(basis_values, aux_values, factors, frag_slot, dimer_pairs, counts, weights, metric_inv)


def solution(mesh):
    placed = (
        P("dimer", "grid", None),
        P("dimer", "grid", None),
        P("dimer", "grid", None),
        P(),
        P("dimer", None),
        P("dimer", "grid"),
        P("dimer", "grid"),
        P("dimer", "grid", None),
    )
    return jax.shard_map(
        shards,
        mesh=mesh,
        in_specs=placed,
        out_specs=(P("dimer", "grid", None), P("dimer", "grid", None)),
        check_vma=False,
    )
```

```python
import functools

import jax
import jax.numpy as jnp
from jax import lax
from jax.experimental import pallas as pl
from jax.experimental.pallas import tpu as pltpu
from jax.sharding import PartitionSpec as P

EXCHANGE_COEFF = 0.9847450218426964
GRID = 32
DIMERS = 8
CHIPS = 16
FAR_GRID = sorted(range(1, 32), key=lambda k: -min(k, 32 - k))
FAR_CHIPS = sorted(range(1, 16), key=lambda k: -min(k, 16 - k))
FAR_Z = sorted(range(1, 8), key=lambda k: -min(k, 8 - k))
FAR_DIMERS = (2, 6, 4, 1, 3, 5, 7)
NC = 256
CHUNKS = (
    (1, 768, "z"), (0, 0, "y"), (0, 256, "y"), (1, 512, "y"), (0, 512, "y"), (0, 768, "y"),
)
SCHEDULE = (
    "o0 w0 o1 w1", "o2 s0 w2 s1", "o3 w3 s2 o4", "w4 s3 o5 w5", "t1 s4 t2 s5",
    "t3 t0 t4 t5",
)
PTS = 1280
FB = 512
OCC = 128
AUX = 2048
F32 = jnp.float32
BF16 = jnp.bfloat16
MESH = pl.DeviceIdType.MESH


def wait_bytes(ref, sem):
    pltpu.make_async_copy(ref, ref, sem).wait()


def remote(src, dst, send_sem, recv_sem, axis, index):
    copy = pltpu.make_async_remote_copy(
        src_ref=src,
        dst_ref=dst,
        send_sem=send_sem,
        recv_sem=recv_sem,
        device_id={axis: index},
        device_id_type=MESH,
    )
    copy.start()


def hi_lo_rows(row):
    high = row.astype(BF16)
    low = (row - high.astype(F32)).astype(BF16)
    which = lax.broadcasted_iota(jnp.int32, (16, row.shape[1]), 0)
    zero = jnp.zeros((16, row.shape[1]), F32)
    high, low = high.astype(F32), low.astype(F32)
    return jnp.where(which == 0, high, jnp.where(which == 1, low, zero)).astype(BF16)


def cube_root(x):
    safe = jnp.where(x > 0, x, 1.0)
    y = jnp.exp(jnp.log(safe) * (1.0 / 3.0))
    y = y - (y - safe / (y * y)) * (1.0 / 3.0)
    return jnp.where(x > 0, y, 0.0)


def dot(a, b):
    return jnp.dot(a, b, preferred_element_type=F32)


def kernel(
    basis_hbm, aux_hbm, fac_ref, slot_ref, pairs_ref, counts_ref, weights_ref, metric_hbm,
    out,
    b, aux, bt, auxt, wt, mbuf, facbuf, facsend, facall,
    ssend, srecv, fsend, frecv, csend, crecv,
    acc, core_send, core_recv, y_send, y_recv, z_send, z_recv,
    w_send, w_recv, v_send, v_recv, d_send, d_recv,
    local_sem, fa_sem, fb_sem, fc_sem, m_sem, s_sem, f_sem, c_sem,
    core_sem, y_sem, z_sem, d_sem,
):
    d = lax.axis_index("dimer")
    g = lax.axis_index("grid")
    core = lax.rem(g, 2)
    chip = g // 2
    y = lax.rem(chip, 2)
    z = chip // 2
    other_core = g + 1 - 2 * core
    other_y = g + 2 - 4 * y

    load_b = pltpu.make_async_copy(basis_hbm.at[0], b, local_sem.at[0])
    load_aux = pltpu.make_async_copy(aux_hbm.at[0], aux, local_sem.at[1])
    load_m = pltpu.make_async_copy(metric_hbm.at[0], mbuf.at[core], local_sem.at[2])
    load_b.start()
    load_aux.start()
    load_m.start()

    barrier = pltpu.get_barrier_semaphore()
    for k in FAR_GRID:
        pl.semaphore_signal(
            barrier, inc=1, device_id={"grid": lax.rem(g + k, GRID)}, device_id_type=MESH
        )
    for k in FAR_DIMERS:
        pl.semaphore_signal(
            barrier, inc=1, device_id={"dimer": lax.rem(d + k, DIMERS)}, device_id_type=MESH
        )
    pl.semaphore_wait(barrier, GRID - 1 + DIMERS - 1)

    for k in FAR_DIMERS:
        remote(
            fac_ref.at[0], facbuf.at[d], fa_sem.at[0], fa_sem.at[1],
            "dimer", lax.rem(d + k, DIMERS),
        )
    facbuf[d] = fac_ref[0]
    remote(metric_hbm.at[0], mbuf.at[core], m_sem.at[0], m_sem.at[1], "grid", other_core)

    position = lax.broadcasted_iota(jnp.int32, (1, PTS), 1)
    lw = jnp.where(position < counts_ref[...], weights_ref[...], 0.0)
    load_aux.wait()
    sums = dot(hi_lo_rows(lw), aux[...])
    sums = sums[0:1, :] + sums[1:2, :]
    for k in range(CHIPS):
        ssend[k] = sums[:, k * 128:(k + 1) * 128]
    srecv[g] = ssend[chip]
    for k in FAR_GRID:
        to = lax.rem(g + k, GRID)
        remote(ssend.at[to // 2], srecv.at[g], s_sem.at[0], s_sem.at[1], "grid", to)

    first, second = pairs_ref[0, 0], pairs_ref[0, 1]
    place = core * 256 + y * 128 + z * 16
    rows = pl.ds(pl.multiple_of(place, 16), 16)
    wait_bytes(facbuf.at[pl.ds(0, DIMERS - 1)], fa_sem.at[1])
    facsend[0] = facbuf[slot_ref[first]]
    facsend[1] = facbuf[slot_ref[second]]
    facall[:, rows, :] = facsend[...]
    for k in FAR_CHIPS:
        remote(
            facsend, facall.at[:, rows, :], fb_sem.at[0], fb_sem.at[1],
            "grid", 2 * lax.rem(chip + k, CHIPS) + core,
        )

    load_b.wait()
    for block in range(8):
        turned = b[:, block * 128:(block + 1) * 128].T
        for part in range(8):
            group = block * 8 + part
            half, owner = group // 32, group % 32
            place = half * 32 + (owner % 2) * 16 + ((owner // 2) % 2) * 8 + owner // 4
            bt[place * 16:(place + 1) * 16, :] = turned[part * 16:(part + 1) * 16, :]

    wait_bytes(facall.at[:, pl.ds(0, 240), :], fb_sem.at[1])
    own_half = pl.ds(pl.multiple_of(core * 256, 256), 256)
    remote(
        facall.at[:, own_half, :], facall.at[:, own_half, :], fc_sem.at[0], fc_sem.at[1],
        "grid", other_core,
    )

    def orbitals(half, of_core):
        rows = pl.ds(pl.multiple_of(of_core * 256, 256), 256)
        at = pl.ds(pl.multiple_of(half * FB + of_core * 256, 256), 256)
        turn = (((0,), (0,)), ((), ()))
        return lax.dot_general(
            facall[half, rows, :], bt[at, :], turn, preferred_element_type=F32
        )

    orb_first, orb_second = orbitals(0, core), orbitals(1, core)
    wait_bytes(facall.at[:, pl.ds(0, 256), :], fc_sem.at[1])
    orb_first += orbitals(0, 1 - core)
    orb_second += orbitals(1, 1 - core)
    density = jnp.sum(orb_first * orb_first + orb_second * orb_second, axis=0, keepdims=True)
    density = density * (1.0 / (2.0 * OCC))
    exchange = -EXCHANGE_COEFF * cube_root(density)

    parts = hi_lo_rows(lw * density)
    for part in range(2):
        fitted = dot(parts, aux[:, part * 1024:(part + 1) * 1024])
        fsend[part] = fitted[0:1, :] + fitted[1:2, :]
        frecv[chip, part] = fsend[part]
        for k in FAR_CHIPS:
            remote(
                fsend.at[part], frecv.at[chip, part], f_sem.at[0], f_sem.at[1],
                "grid", 2 * lax.rem(chip + k, CHIPS) + core,
            )
    for k in range(CHIPS):
        auxt[k * 128:(k + 1) * 128, :] = aux[:, k * 128:(k + 1) * 128].T

    local_exchange = jnp.sum(lw * exchange, axis=1, keepdims=True)
    local_weight = jnp.sum(lw, axis=1, keepdims=True)
    wait_bytes(srecv.at[pl.ds(0, GRID - 1)], s_sem.at[1])
    s_total = jnp.sum(srecv[...], axis=0)
    load_m.wait()
    wait_bytes(mbuf.at[0], m_sem.at[1])
    wait_bytes(frecv.at[pl.ds(0, CHIPS - 1)], f_sem.at[1])
    own_fitted = jnp.sum(frecv[...], axis=0)
    own_fitted = jnp.concatenate([own_fitted[0], own_fitted[1]], axis=1)

    rows_m = jnp.concatenate([mbuf[0], mbuf[1]], axis=0)
    terms = rows_m[:, 0:128] * own_fitted[:, 0:128]
    for k in range(1, CHIPS):
        cols = slice(k * 128, (k + 1) * 128)
        terms += rows_m[:, cols] * own_fitted[:, cols]
    coef_part = jnp.sum(terms.T, axis=0, keepdims=True)
    total_part = jnp.sum(coef_part * s_total, axis=1, keepdims=True) + local_exchange
    lane = lax.broadcasted_iota(jnp.int32, (1, 128), 1)
    csend[0:1, :] = coef_part
    csend[1:2, :] = jnp.where(lane == 0, total_part, jnp.where(lane == 1, local_weight, 0.0))
    crecv[g] = csend[...]
    for k in FAR_GRID:
        remote(
            csend, crecv.at[g], c_sem.at[0], c_sem.at[1], "grid", lax.rem(g + k, GRID)
        )
    wait_bytes(crecv.at[pl.ds(0, GRID - 1)], c_sem.at[1])

    totals = jnp.sum(crecv[...], axis=0)[1:2, :]
    average = totals[:, 0:1] / totals[:, 1:2]
    coefficients = jnp.concatenate(
        [crecv[2 * k, 0:1, :] + crecv[2 * k + 1, 0:1, :] for k in range(CHIPS)], axis=1
    )
    coulomb = dot(hi_lo_rows(coefficients), auxt[...])
    coulomb = coulomb[0:1, :] + coulomb[1:2, :]
    potential = lw * (coulomb + exchange - average)
    weighted = set()

    def product(chunk, other):
        half, column, _ = CHUNKS[chunk]
        of_core = 1 - core if other else core
        at = pl.ds(pl.multiple_of(half * FB + of_core * 256, 256), 256)
        if (half, other) not in weighted:
            weighted.add((half, other))
            wt[at, :] = (bt[at, :].astype(F32) * potential).astype(BF16)
        return dot(wt[at, :], b[:, column:column + NC])

    here = pl.ds(pl.multiple_of(y * 128, 128), 128)
    there = pl.ds(pl.multiple_of((1 - y) * 128, 128), 128)
    own_z = pl.ds(pl.multiple_of(z * 16, 16), 16)
    own_rows = pl.ds(pl.multiple_of(y * 128 + z * 16, 16), 16)
    there_rows = pl.ds(pl.multiple_of((1 - y) * 128 + z * 16, 16), 16)
    z_peers = [(k, lax.rem(z + k, 8)) for k in FAR_Z]

    def other_product(chunk):
        core_send[chunk] = product(chunk, True)
        remote(
            core_send.at[chunk], core_recv.at[chunk],
            core_sem.at[0, chunk], core_sem.at[1, chunk], "grid", other_core,
        )

    def own_product(chunk):
        acc[chunk] = product(chunk, False)

    def first_sum(chunk):
        wait_bytes(core_recv.at[chunk], core_sem.at[1, chunk])
        if CHUNKS[chunk][2] == "y":
            y_send[chunk] = (acc[chunk, there, :] + core_recv[chunk, there, :]).astype(BF16)
            remote(
                y_send.at[chunk], y_recv.at[chunk],
                y_sem.at[0, chunk], y_sem.at[1, chunk], "grid", other_y,
            )
            acc[chunk, here, :] += core_recv[chunk, here, :]
        else:
            acc[chunk] += core_recv[chunk]
            for line in range(2):
                for part in range(8):
                    row = line * 128 + part * 16
                    w_send[chunk, part, line] = acc[chunk, row:row + 16, :].astype(BF16)
            for k, to in z_peers:
                remote(
                    w_send.at[chunk, to], w_recv.at[chunk, k - 1],
                    z_sem.at[0, chunk], z_sem.at[1, chunk], "grid", to * 4 + y * 2 + core,
                )

    def second_sum(chunk):
        if CHUNKS[chunk][2] == "y":
            wait_bytes(y_recv.at[chunk], y_sem.at[1, chunk])
            acc[chunk, here, :] += y_recv[chunk].astype(F32)
            z_send[chunk] = acc[chunk, here, :].astype(BF16)
            for k, to in z_peers:
                at = pl.ds(pl.multiple_of(to * 16, 16), 16)
                remote(
                    z_send.at[chunk, at, :], z_recv.at[chunk, k - 1],
                    z_sem.at[0, chunk], z_sem.at[1, chunk], "grid", to * 4 + y * 2 + core,
                )
        else:
            wait_bytes(w_recv.at[chunk], z_sem.at[1, chunk])
            mine, theirs = acc[chunk, own_rows, :], acc[chunk, there_rows, :]
            for k in range(7):
                mine = mine + w_recv[chunk, k, y].astype(F32)
                theirs = theirs + w_recv[chunk, k, 1 - y].astype(F32)
            acc[chunk, own_rows, :] = mine
            v_send[chunk] = theirs.astype(BF16)
            remote(
                v_send.at[chunk], v_recv.at[chunk],
                y_sem.at[0, chunk], y_sem.at[1, chunk], "grid", other_y,
            )

    done = {}

    def ended(chunk):
        own = acc[chunk, own_rows, :]
        if CHUNKS[chunk][2] == "y":
            wait_bytes(z_recv.at[chunk], z_sem.at[1, chunk])
            for k in range(7):
                own = own + z_recv[chunk, k].astype(F32)
        else:
            wait_bytes(v_recv.at[chunk], y_sem.at[1, chunk])
            own = own + v_recv[chunk].astype(F32)
        done[chunk] = own

    steps = {"o": other_product, "w": own_product, "s": first_sum, "t": second_sum, "e": ended}
    for step in " ".join(SCHEDULE).split():
        steps[step[0]](int(step[1:]))

    def share(half, column):
        chunks = [i for i, c in enumerate(CHUNKS) if c[0] == half and c[1] // FB == column]
        for chunk in chunks:
            if chunk not in done:
                ended(chunk)
        return jnp.concatenate([done[i] for i in sorted(chunks, key=lambda i: CHUNKS[i][1])], axis=1)

    own_first, own_second = share(0, 0), share(1, 1)

    def for_fragment(index):
        return jnp.where(first == index, own_first, 0.0) + jnp.where(
            second == index, own_second, 0.0
        )

    for k in FAR_DIMERS:
        to = lax.rem(d + k, DIMERS)
        d_send[k - 1] = for_fragment(to)
        remote(
            d_send.at[k - 1], d_recv.at[k - 1], d_sem.at[0], d_sem.at[1], "dimer", to
        )
    own = for_fragment(d)
    out[1] = share(0, 1)
    wait_bytes(d_recv, d_sem.at[1])
    for k in range(DIMERS - 1):
        own = own + d_recv[k]
    out[0] = own

    wait_bytes(facbuf.at[pl.ds(0, DIMERS - 1)], fa_sem.at[0])
    wait_bytes(mbuf.at[0], m_sem.at[0])
    wait_bytes(facall.at[:, pl.ds(0, 240), :], fb_sem.at[0])
    wait_bytes(facall.at[:, pl.ds(0, 256), :], fc_sem.at[0])
    wait_bytes(srecv.at[pl.ds(0, GRID - 1)], s_sem.at[0])
    wait_bytes(frecv.at[pl.ds(0, CHIPS - 1)], f_sem.at[0])
    wait_bytes(crecv.at[pl.ds(0, GRID - 1)], c_sem.at[0])
    for chunk in range(len(CHUNKS)):
        y_first = CHUNKS[chunk][2] == "y"
        wait_bytes(core_recv.at[chunk], core_sem.at[0, chunk])
        wait_bytes((y_recv if y_first else v_recv).at[chunk], y_sem.at[0, chunk])
        wait_bytes((z_recv if y_first else w_recv).at[chunk], z_sem.at[0, chunk])
    wait_bytes(d_recv, d_sem.at[0])


def hand_out(both, frag_out, coup_out):
    frag_out[0] = both[0]
    coup_out[0] = both[1]


def shards(basis_values, aux_values, factors, frag_slot, dimer_pairs, counts, weights, metric_inv):
    vmem = pl.BlockSpec(memory_space=pltpu.VMEM)
    smem = pl.BlockSpec(memory_space=pltpu.SMEM)
    hbm = pl.BlockSpec(memory_space=pl.ANY)
    dma = pltpu.SemaphoreType.DMA
    n = len(CHUNKS)
    share = jax.ShapeDtypeStruct((1, FB // GRID, FB), F32)
    both = pl.pallas_call(
        kernel,
        name="fock",
        out_shape=jax.ShapeDtypeStruct((2, FB // GRID, FB), F32),
        in_specs=[hbm, hbm, vmem, smem, smem, vmem, vmem, hbm],
        out_specs=vmem,
        scratch_shapes=[
            pltpu.VMEM((PTS, 2 * FB), BF16),
            pltpu.VMEM((PTS, AUX), BF16),
            pltpu.VMEM((2 * FB, PTS), BF16),
            pltpu.VMEM((AUX, PTS), BF16),
            pltpu.VMEM((2 * FB, PTS), BF16),
            pltpu.VMEM((2, AUX // GRID, AUX), F32),
            pltpu.VMEM((DIMERS, FB // GRID, OCC), BF16),
            pltpu.VMEM((2, FB // GRID, OCC), BF16),
            pltpu.VMEM((2, FB, OCC), BF16),
            pltpu.VMEM((CHIPS, 1, 128), F32),
            pltpu.VMEM((GRID, 1, 128), F32),
            pltpu.VMEM((2, 1, AUX // 2), F32),
            pltpu.VMEM((CHIPS, 2, 1, AUX // 2), F32),
            pltpu.VMEM((2, 128), F32),
            pltpu.VMEM((GRID, 2, 128), F32),
            pltpu.VMEM((n, 256, NC), F32),
            pltpu.VMEM((n, 256, NC), F32),
            pltpu.VMEM((n, 256, NC), F32),
            pltpu.VMEM((n, 128, NC), BF16),
            pltpu.VMEM((n, 128, NC), BF16),
            pltpu.VMEM((n, 128, NC), BF16),
            pltpu.VMEM((n, 7, 16, NC), BF16),
            pltpu.VMEM((n, 8, 2, 16, NC), BF16),
            pltpu.VMEM((n, 7, 2, 16, NC), BF16),
            pltpu.VMEM((n, 16, NC), BF16),
            pltpu.VMEM((n, 16, NC), BF16),
            pltpu.VMEM((DIMERS - 1, 16, FB), F32),
            pltpu.VMEM((DIMERS - 1, 16, FB), F32),
            dma((3,)), dma((2,)), dma((2,)), dma((2,)), dma((2,)), dma((2,)), dma((2,)), dma((2,)),
            dma((2, n)), dma((2, n)), dma((2, n)), dma((2,)),
        ],
        compiler_params=pltpu.CompilerParams(
            collective_id=0, has_side_effects=True, vmem_limit_bytes=60 * 1024 * 1024
        ),
        cost_estimate=pl.CostEstimate(
            flops=2 * PTS * (2 * FB * OCC + 3 * AUX + 3 * FB * FB),
            bytes_accessed=2 * PTS * (2 * FB + AUX) + 4 * AUX * AUX // GRID,
            transcendentals=2 * PTS,
        ),
    )(basis_values, aux_values, factors, frag_slot, dimer_pairs, counts, weights, metric_inv)
    return pl.pallas_call(
        hand_out,
        name="outputs",
        out_shape=(share, share),
        in_specs=[vmem],
        out_specs=(vmem, vmem),
    )(both)


def solution(mesh):
    placed = (
        P("dimer", "grid", None),
        P("dimer", "grid", None),
        P("dimer", "grid", None),
        P(),
        P("dimer", None),
        P("dimer", "grid"),
        P("dimer", "grid"),
        P("dimer", "grid", None),
    )
    return jax.shard_map(
        shards,
        mesh=mesh,
        in_specs=placed,
        out_specs=(P("dimer", "grid", None), P("dimer", "grid", None)),
        check_vma=False,
    )
```

```python
import functools

import jax
import jax.numpy as jnp
from jax import lax
from jax.experimental import pallas as pl
from jax.experimental.pallas import tpu as pltpu
from jax.sharding import PartitionSpec as P

EXCHANGE_COEFF = 0.9847450218426964
GRID = 32
DIMERS = 8
CHIPS = 16
FAR_GRID = sorted(range(1, 32), key=lambda k: -min(k, 32 - k))
FAR_CHIPS = sorted(range(1, 16), key=lambda k: -min(k, 16 - k))
FAR_Z = sorted(range(1, 8), key=lambda k: -min(k, 8 - k))
FAR_DIMERS = (2, 6, 4, 1, 3, 5, 7)
CHUNKS = (
    (1, 768, 256, "z"),
    (0, 0, 256, "y"),
    (0, 256, 256, "y"),
    (1, 512, 256, "y"),
    (0, 512, 256, "y"),
    (0, 768, 256, "y"),
)
SCHEDULE = (
    "o0 w0 o1 w1", "o2 s0 w2 s1", "o3 w3 s2 o4", "w4 s3 o5 w5", "t1 s4 t2 s5",
    "t3 t0 t4 t5",
)
PTS = 1280
FB = 512
OCC = 128
AUX = 2048
F32 = jnp.float32
BF16 = jnp.bfloat16
MESH = pl.DeviceIdType.MESH


def wait_bytes(ref, sem):
    pltpu.make_async_copy(ref, ref, sem).wait()


def remote(src, dst, send_sem, recv_sem, axis, index):
    copy = pltpu.make_async_remote_copy(
        src_ref=src,
        dst_ref=dst,
        send_sem=send_sem,
        recv_sem=recv_sem,
        device_id={axis: index},
        device_id_type=MESH,
    )
    copy.start()


def hi_lo_rows(row):
    high = row.astype(BF16)
    low = (row - high.astype(F32)).astype(BF16)
    which = lax.broadcasted_iota(jnp.int32, (16, row.shape[1]), 0)
    zero = jnp.zeros((16, row.shape[1]), F32)
    high, low = high.astype(F32), low.astype(F32)
    return jnp.where(which == 0, high, jnp.where(which == 1, low, zero)).astype(BF16)


def cube_root(x):
    safe = jnp.where(x > 0, x, 1.0)
    y = jnp.exp(jnp.log(safe) * (1.0 / 3.0))
    y = y - (y - safe / (y * y)) * (1.0 / 3.0)
    return jnp.where(x > 0, y, 0.0)


def dot(a, b):
    return jnp.dot(a, b, preferred_element_type=F32)


def kernel(
    basis_hbm, aux_hbm, fac_hbm, slot_hbm, pairs_hbm, counts_hbm, weights_hbm, metric_hbm,
    out,
    slot_ref, pairs_ref, counts_ref, weights_ref, b, aux, bt, auxt, wt, mbuf, facbuf, facsend, facall,
    ssend, srecv, fsend, frecv, csend, crecv,
    acc, core_send, core_recv, y_send, y_recv, z_send, z_recv,
    w_send, w_recv, v_send, v_recv, d_send, d_recv,
    local_sem, fa_sem, fb_sem, fc_sem, m_sem, s_sem, f_sem, c_sem,
    core_sem, y_sem, z_sem, d_sem,
):
    d = lax.axis_index("dimer")
    g = lax.axis_index("grid")
    core = lax.rem(g, 2)
    chip = g // 2
    y = lax.rem(chip, 2)
    z = chip // 2
    other_core = g + 1 - 2 * core
    other_y = g + 2 - 4 * y

    barrier = pltpu.get_barrier_semaphore()
    for k in FAR_GRID:
        pl.semaphore_signal(
            barrier, inc=1, device_id={"grid": lax.rem(g + k, GRID)}, device_id_type=MESH
        )
    for k in FAR_DIMERS:
        pl.semaphore_signal(
            barrier, inc=1, device_id={"dimer": lax.rem(d + k, DIMERS)}, device_id_type=MESH
        )
    load_b = pltpu.make_async_copy(basis_hbm.at[0], b, local_sem.at[0])
    load_aux = pltpu.make_async_copy(aux_hbm.at[0], aux, local_sem.at[1])
    load_m = pltpu.make_async_copy(metric_hbm.at[0], mbuf.at[core], local_sem.at[2])
    load_b.start()
    load_aux.start()
    load_m.start()
    load_small = [
        pltpu.make_async_copy(source, place, local_sem.at[3 + at])
        for at, (source, place) in enumerate((
            (slot_hbm, slot_ref), (pairs_hbm, pairs_ref), (counts_hbm, counts_ref),
            (weights_hbm, weights_ref), (fac_hbm.at[0], facbuf.at[d]),
        ))
    ]
    for load in load_small:
        load.start()
    pl.semaphore_wait(barrier, GRID - 1 + DIMERS - 1)

    for k in FAR_DIMERS:
        remote(
            fac_hbm.at[0], facbuf.at[d], fa_sem.at[0], fa_sem.at[1],
            "dimer", lax.rem(d + k, DIMERS),
        )
    remote(metric_hbm.at[0], mbuf.at[core], m_sem.at[0], m_sem.at[1], "grid", other_core)

    for load in load_small:
        load.wait()
    position = lax.broadcasted_iota(jnp.int32, (1, PTS), 1)
    lw = jnp.where(position < counts_ref[...], weights_ref[...], 0.0)
    load_aux.wait()
    sums = dot(hi_lo_rows(lw), aux[...])
    sums = sums[0:1, :] + sums[1:2, :]
    for k in range(CHIPS):
        ssend[k] = sums[:, k * 128:(k + 1) * 128]
    srecv[g] = ssend[chip]
    for k in FAR_GRID:
        to = lax.rem(g + k, GRID)
        remote(ssend.at[to // 2], srecv.at[g], s_sem.at[0], s_sem.at[1], "grid", to)

    first, second = pairs_ref[0, 0], pairs_ref[0, 1]
    place = core * 256 + y * 128 + z * 16
    rows = pl.ds(pl.multiple_of(place, 16), 16)
    wait_bytes(facbuf.at[pl.ds(0, DIMERS - 1)], fa_sem.at[1])
    facsend[0] = facbuf[slot_ref[first]]
    facsend[1] = facbuf[slot_ref[second]]
    facall[:, rows, :] = facsend[...]
    for k in FAR_CHIPS:
        remote(
            facsend, facall.at[:, rows, :], fb_sem.at[0], fb_sem.at[1],
            "grid", 2 * lax.rem(chip + k, CHIPS) + core,
        )

    load_b.wait()
    for block in range(8):
        turned = b[:, block * 128:(block + 1) * 128].T
        for part in range(8):
            group = block * 8 + part
            half, owner = group // 32, group % 32
            place = half * 32 + (owner % 2) * 16 + ((owner // 2) % 2) * 8 + owner // 4
            bt[place * 16:(place + 1) * 16, :] = turned[part * 16:(part + 1) * 16, :]

    wait_bytes(facall.at[:, pl.ds(0, 240), :], fb_sem.at[1])
    own_half = pl.ds(pl.multiple_of(core * 256, 256), 256)
    remote(
        facall.at[:, own_half, :], facall.at[:, own_half, :], fc_sem.at[0], fc_sem.at[1],
        "grid", other_core,
    )

    def orbitals(half, of_core):
        rows = pl.ds(pl.multiple_of(of_core * 256, 256), 256)
        at = pl.ds(pl.multiple_of(half * FB + of_core * 256, 256), 256)
        turn = (((0,), (0,)), ((), ()))
        return lax.dot_general(
            facall[half, rows, :], bt[at, :], turn, preferred_element_type=F32
        )

    orb_first, orb_second = orbitals(0, core), orbitals(1, core)
    wait_bytes(facall.at[:, pl.ds(0, 256), :], fc_sem.at[1])
    orb_first += orbitals(0, 1 - core)
    orb_second += orbitals(1, 1 - core)
    density = jnp.sum(orb_first * orb_first + orb_second * orb_second, axis=0, keepdims=True)
    density = density * (1.0 / (2.0 * OCC))
    exchange = -EXCHANGE_COEFF * cube_root(density)

    parts = hi_lo_rows(lw * density)
    fitted = dot(parts, aux[...])
    fitted = fitted[0:1, :] + fitted[1:2, :]
    fsend[0] = fitted[:, 0:1024]
    fsend[1] = fitted[:, 1024:2048]
    frecv[chip] = fsend[...]
    if True:
        for k in FAR_CHIPS:
            remote(
                fsend, frecv.at[chip], f_sem.at[0], f_sem.at[1],
                "grid", 2 * lax.rem(chip + k, CHIPS) + core,
            )
    for k in range(CHIPS):
        auxt[k * 128:(k + 1) * 128, :] = aux[:, k * 128:(k + 1) * 128].T

    local_exchange = jnp.sum(lw * exchange, axis=1, keepdims=True)
    local_weight = jnp.sum(lw, axis=1, keepdims=True)
    wait_bytes(srecv.at[pl.ds(0, GRID - 1)], s_sem.at[1])
    s_total = jnp.sum(srecv[...], axis=0)
    load_m.wait()
    wait_bytes(mbuf.at[0], m_sem.at[1])
    wait_bytes(frecv.at[pl.ds(0, CHIPS - 1)], f_sem.at[1])
    own_fitted = jnp.sum(frecv[...], axis=0)
    own_fitted = jnp.concatenate([own_fitted[0], own_fitted[1]], axis=1)

    rows_m = jnp.concatenate([mbuf[0], mbuf[1]], axis=0)
    terms = rows_m[:, 0:128] * own_fitted[:, 0:128]
    for k in range(1, CHIPS):
        cols = slice(k * 128, (k + 1) * 128)
        terms += rows_m[:, cols] * own_fitted[:, cols]
    coef_part = jnp.sum(terms.T, axis=0, keepdims=True)
    total_part = jnp.sum(coef_part * s_total, axis=1, keepdims=True) + local_exchange
    lane = lax.broadcasted_iota(jnp.int32, (1, 128), 1)
    csend[0:1, :] = coef_part
    csend[1:2, :] = jnp.where(lane == 0, total_part, jnp.where(lane == 1, local_weight, 0.0))
    crecv[g] = csend[...]
    for k in FAR_GRID:
        remote(
            csend, crecv.at[g], c_sem.at[0], c_sem.at[1], "grid", lax.rem(g + k, GRID)
        )
    wait_bytes(crecv.at[pl.ds(0, GRID - 1)], c_sem.at[1])

    totals = jnp.sum(crecv[...], axis=0)[1:2, :]
    average = totals[:, 0:1] / totals[:, 1:2]
    coefficients = jnp.concatenate(
        [crecv[2 * k, 0:1, :] + crecv[2 * k + 1, 0:1, :] for k in range(CHIPS)], axis=1
    )
    coulomb = dot(hi_lo_rows(coefficients), auxt[...])
    coulomb = coulomb[0:1, :] + coulomb[1:2, :]
    potential = lw * (coulomb + exchange - average)
    weighted = set()

    def product(chunk, other):
        half, column, wide, _ = CHUNKS[chunk]
        of_core = 1 - core if other else core
        at = pl.ds(pl.multiple_of(half * FB + of_core * 256, 256), 256)
        if (half, other) not in weighted:
            weighted.add((half, other))
            wt[at, :] = (bt[at, :].astype(F32) * potential).astype(BF16)
        return dot(wt[at, :], b[:, column:column + wide])

    here = pl.ds(pl.multiple_of(y * 128, 128), 128)
    there = pl.ds(pl.multiple_of((1 - y) * 128, 128), 128)
    own_z = pl.ds(pl.multiple_of(z * 16, 16), 16)
    own_rows = pl.ds(pl.multiple_of(y * 128 + z * 16, 16), 16)
    there_rows = pl.ds(pl.multiple_of((1 - y) * 128 + z * 16, 16), 16)
    z_peers = [(k, lax.rem(z + k, 8)) for k in FAR_Z]

    def other_product(chunk):
        core_send[chunk][...] = product(chunk, True)
        remote(
            core_send[chunk], core_recv[chunk],
            core_sem.at[0, chunk], core_sem.at[1, chunk], "grid", other_core,
        )

    def own_product(chunk):
        acc[chunk][...] = product(chunk, False)

    def first_sum(chunk):
        wait_bytes(core_recv[chunk], core_sem.at[1, chunk])
        if CHUNKS[chunk][3] == "y":
            y_send[chunk][...] = (acc[chunk][there, :] + core_recv[chunk][there, :]).astype(BF16)
            remote(
                y_send[chunk], y_recv[chunk],
                y_sem.at[0, chunk], y_sem.at[1, chunk], "grid", other_y,
            )
            acc[chunk][here, :] += core_recv[chunk][here, :]
        else:
            acc[chunk][...] += core_recv[chunk][...]
            for line in range(2):
                for part in range(8):
                    row = line * 128 + part * 16
                    w_send[chunk][part, line] = acc[chunk][row:row + 16, :].astype(BF16)
            for k, to in z_peers:
                remote(
                    w_send[chunk].at[to], w_recv[chunk].at[k - 1],
                    z_sem.at[0, chunk], z_sem.at[1, chunk], "grid", to * 4 + y * 2 + core,
                )

    def second_sum(chunk):
        if CHUNKS[chunk][3] == "y":
            wait_bytes(y_recv[chunk], y_sem.at[1, chunk])
            acc[chunk][here, :] += y_recv[chunk][...].astype(F32)
            z_send[chunk][...] = acc[chunk][here, :].astype(BF16)
            for k, to in z_peers:
                at = pl.ds(pl.multiple_of(to * 16, 16), 16)
                remote(
                    z_send[chunk].at[at, :], z_recv[chunk].at[k - 1],
                    z_sem.at[0, chunk], z_sem.at[1, chunk], "grid", to * 4 + y * 2 + core,
                )
        else:
            wait_bytes(w_recv[chunk], z_sem.at[1, chunk])
            mine, theirs = acc[chunk][own_rows, :], acc[chunk][there_rows, :]
            for k in range(7):
                mine = mine + w_recv[chunk][k, y].astype(F32)
                theirs = theirs + w_recv[chunk][k, 1 - y].astype(F32)
            acc[chunk][own_rows, :] = mine
            v_send[chunk][...] = theirs.astype(BF16)
            remote(
                v_send[chunk], v_recv[chunk],
                y_sem.at[0, chunk], y_sem.at[1, chunk], "grid", other_y,
            )

    done = {}

    def ended(chunk):
        own = acc[chunk][own_rows, :]
        if CHUNKS[chunk][3] == "y":
            wait_bytes(z_recv[chunk], z_sem.at[1, chunk])
            for k in range(7):
                own = own + z_recv[chunk][k].astype(F32)
        else:
            wait_bytes(v_recv[chunk], y_sem.at[1, chunk])
            own = own + v_recv[chunk][...].astype(F32)
        done[chunk] = own

    steps = {"o": other_product, "w": own_product, "s": first_sum, "t": second_sum, "e": ended}
    for step in " ".join(SCHEDULE).split():
        steps[step[0]](int(step[1:]))

    def share(half, column):
        chunks = [i for i, c in enumerate(CHUNKS) if c[0] == half and c[1] // FB == column]
        for chunk in chunks:
            if chunk not in done:
                ended(chunk)
        return jnp.concatenate([done[i] for i in sorted(chunks, key=lambda i: CHUNKS[i][1])], axis=1)

    own_first, own_second = share(0, 0), share(1, 1)

    def for_fragment(index):
        return jnp.where(first == index, own_first, 0.0) + jnp.where(
            second == index, own_second, 0.0
        )

    for k in FAR_DIMERS:
        to = lax.rem(d + k, DIMERS)
        d_send[k - 1] = for_fragment(to)
        remote(
            d_send.at[k - 1], d_recv.at[k - 1], d_sem.at[0], d_sem.at[1], "dimer", to
        )
    own = for_fragment(d)
    out[1] = share(0, 1)
    wait_bytes(d_recv, d_sem.at[1])
    for k in range(DIMERS - 1):
        own = own + d_recv[k]
    out[0] = own

    wait_bytes(facbuf.at[pl.ds(0, DIMERS - 1)], fa_sem.at[0])
    wait_bytes(mbuf.at[0], m_sem.at[0])
    wait_bytes(facall.at[:, pl.ds(0, 240), :], fb_sem.at[0])
    wait_bytes(facall.at[:, pl.ds(0, 256), :], fc_sem.at[0])
    wait_bytes(srecv.at[pl.ds(0, GRID - 1)], s_sem.at[0])
    wait_bytes(frecv.at[pl.ds(0, CHIPS - 1)], f_sem.at[0])
    wait_bytes(crecv.at[pl.ds(0, GRID - 1)], c_sem.at[0])
    for chunk in range(len(CHUNKS)):
        y_first = CHUNKS[chunk][3] == "y"
        wait_bytes(core_recv[chunk], core_sem.at[0, chunk])
        wait_bytes((y_recv if y_first else v_recv)[chunk], y_sem.at[0, chunk])
        wait_bytes((z_recv if y_first else w_recv)[chunk], z_sem.at[0, chunk])
    wait_bytes(d_recv, d_sem.at[0])


def shards(basis_values, aux_values, factors, frag_slot, dimer_pairs, counts, weights, metric_inv):
    vmem = pl.BlockSpec(memory_space=pltpu.VMEM)
    smem = pl.BlockSpec(memory_space=pltpu.SMEM)
    hbm = pl.BlockSpec(memory_space=pl.ANY)
    dma = pltpu.SemaphoreType.DMA
    n = len(CHUNKS)

    def per_chunk(shape, dtype):
        return [pltpu.VMEM((*shape, chunk[2]), dtype) for chunk in CHUNKS]

    both = pl.pallas_call(
        kernel,
        name="fock",
        out_shape=pltpu.VMEM((2, FB // GRID, FB), F32),
        in_specs=[hbm] * 8,
        out_specs=vmem,
        scratch_shapes=[
            pltpu.SMEM((DIMERS,), jnp.int32),
            pltpu.SMEM((1, 2), jnp.int32),
            pltpu.VMEM((1, 1), jnp.int32),
            pltpu.VMEM((1, PTS), F32),
            pltpu.VMEM((PTS, 2 * FB), BF16),
            pltpu.VMEM((PTS, AUX), BF16),
            pltpu.VMEM((2 * FB, PTS), BF16),
            pltpu.VMEM((AUX, PTS), BF16),
            pltpu.VMEM((2 * FB, PTS), BF16),
            pltpu.VMEM((2, AUX // GRID, AUX), F32),
            pltpu.VMEM((DIMERS, FB // GRID, OCC), BF16),
            pltpu.VMEM((2, FB // GRID, OCC), BF16),
            pltpu.VMEM((2, FB, OCC), BF16),
            pltpu.VMEM((CHIPS, 1, 128), F32),
            pltpu.VMEM((GRID, 1, 128), F32),
            pltpu.VMEM((2, 1, AUX // 2), F32),
            pltpu.VMEM((CHIPS, 2, 1, AUX // 2), F32),
            pltpu.VMEM((2, 128), F32),
            pltpu.VMEM((GRID, 2, 128), F32),
            per_chunk((256,), F32),
            per_chunk((256,), F32),
            per_chunk((256,), F32),
            per_chunk((128,), BF16),
            per_chunk((128,), BF16),
            per_chunk((128,), BF16),
            per_chunk((7, 16), BF16),
            per_chunk((8, 2, 16), BF16),
            per_chunk((7, 2, 16), BF16),
            per_chunk((16,), BF16),
            per_chunk((16,), BF16),
            pltpu.VMEM((DIMERS - 1, 16, FB), F32),
            pltpu.VMEM((DIMERS - 1, 16, FB), F32),
            dma((8,)), dma((2,)), dma((2,)), dma((2,)), dma((2,)), dma((2,)), dma((2,)), dma((2,)),
            dma((2, n)), dma((2, n)), dma((2, n)), dma((2,)),
        ],
        compiler_params=pltpu.CompilerParams(
            collective_id=0, has_side_effects=True, vmem_limit_bytes=56 * 1024 * 1024
        ),
        cost_estimate=pl.CostEstimate(
            flops=2 * PTS * (2 * FB * OCC + 3 * AUX + 3 * FB * FB),
            bytes_accessed=2 * PTS * (2 * FB + AUX) + 4 * AUX * AUX // GRID,
            transcendentals=2 * PTS,
        ),
    )(basis_values, aux_values, factors, frag_slot, dimer_pairs, counts, weights, metric_inv)
    return both[0:1], both[1:2]


def solution(mesh):
    placed = (
        P("dimer", "grid", None),
        P("dimer", "grid", None),
        P("dimer", "grid", None),
        P(),
        P("dimer", None),
        P("dimer", "grid"),
        P("dimer", "grid"),
        P("dimer", "grid", None),
    )
    return jax.shard_map(
        shards,
        mesh=mesh,
        in_specs=placed,
        out_specs=(P("dimer", "grid", None), P("dimer", "grid", None)),
        check_vma=False,
    )
```
